256 devices in a mesh: tm: 4 (over y_lo, core), pts: 64 (over y_hi, z, x).
Axes of the slice: x: 4, y: 4 (y_hi: 2, y_lo: 2; y = y_hi * 2 + y_lo), z: 8, core: 2. Of those that a mesh axis runs over, the one named last changes fastest.
Arguments:
- saved_paths: bfloat16 [4096, 64, 512], P('tm', 'pts')
- pca_basis: bfloat16 [4096, 4096], P('pts', 'tm')
- vol_surface: float32 [4096, 512], P('tm'), may hold values from 0.5 to 2
- chol_factor: bfloat16 [512, 512], replicated
- exposure_load: float32 [32, 512], replicated, may hold values from -0.25 to 0.25
- reset_load: float32 [32, 512], replicated, may hold values from -0.0234375 to 0.0234375
- strikes: float32 [32], replicated, may hold values from -4 to 4
- bucket_weight: float32 [32], replicated, may hold values from 0.5 to 2
- bucket_start: int32 [32], replicated, may hold values from 0 to 4095, as said below
- generator: int32 [512], replicated, may hold values from 1 to 1048575
- point_ids: int32 [64], P('pts'), may hold values from 0 to 1048575
Outputs:
- normal_adjoint: float32 [4096, 64, 512], P('tm', 'pts')
- vol_greeks: float32 [4096, 512], P('tm')
- chol_greeks: float32 [512, 512], replicated
The draws below stay inside these ranges and needn't reach their ends.
Inputs may be any that keep to these rules, and one draw needn't show every extreme that they name: bucket_start[0] = 0, the last entry is 4095, and the entries rise strictly.
All inputs are finite; a program needn't handle non-finite values.
Results may differ from the reference program's by a relative error of at most 0.0042.
Values may be sent and summed in bfloat16 or wider, within the bound.
No kernel may reach another device: no remote copies, remote signals or barrier semaphores. Data moves between devices by JAX's collectives and lax.ppermute only.
A program may use at most 128 MiB of HBM per device.

```python
import math
import jax
import jax.numpy as jnp
from jax import lax

F = 512
NT = 4096
NE = 32
POINTS = 64


def draw_saved_paths(key, part):
    key = jax.random.fold_in(key, 11)
    growth = jnp.sqrt((jnp.arange(NT, dtype=jnp.float32) + 1.0) / NT)[:, None, None]
    base = jax.random.normal(key, (NT, POINTS, F), jnp.float32)
    return (base * growth).astype(jnp.bfloat16)


def draw_pca_basis(key, part):
    key = jax.random.fold_in(key, 12)
    key_gain, key_rough = jax.random.split(key)
    k_index = jnp.arange(NT, dtype=jnp.int32)[:, None]
    t_index = jnp.arange(NT, dtype=jnp.int32)[None, :]
    phase = (2 * k_index + 1) * (t_index + 1) % (2 * (2 * NT + 1))
    angle = math.pi * phase.astype(jnp.float32) / (2 * NT + 1)
    wave = math.sqrt(2.0 / (NT + 0.5)) * jnp.sin(angle)
    gains = jnp.exp(jax.random.uniform(key_gain, (NT, 1), jnp.float32, math.log(0.3), math.log(3.0)))
    rough = jax.random.normal(key_rough, (NT, NT), jnp.float32)
    entries = wave + 0.8 / math.sqrt(NT) * rough
    return (entries * gains).astype(jnp.bfloat16)


def draw_chol_factor(key, part):
    key = jax.random.fold_in(key, 13)
    key_off, key_diag = jax.random.split(key)
    row_index = jnp.arange(F, dtype=jnp.int32)[:, None]
    col_index = jnp.arange(F, dtype=jnp.int32)[None, :]
    base = jax.random.normal(key_off, (F, F), jnp.float32)
    below = jnp.where(col_index < row_index, base / jnp.sqrt(row_index.astype(jnp.float32) + 1.0), 0.0)
    diag_gain = jax.random.uniform(key_diag, (F, 1), jnp.float32, 0.8, 1.2)
    return (below + jnp.where(col_index == row_index, diag_gain, 0.0)).astype(jnp.bfloat16)


def draw_bucket_start(key, part):
    key = jax.random.fold_in(key, 14)
    picks = jax.random.permutation(key, NT - 2)[:NE - 2] + 1
    middle = jnp.sort(picks).astype(jnp.int32)
    return jnp.concatenate([jnp.zeros((1,), jnp.int32), middle, jnp.full((1,), NT - 1, jnp.int32)])


def with_ends(values, own_key, least, top_value):
    index_at = [jax.random.randint(jax.random.fold_in(own_key, axis), (), 0, length) for axis, length in enumerate(values.shape)]
    longest = values.shape.index(max(values.shape))
    next_to = index_at[:longest] + [(index_at[longest] + 1) % values.shape[longest]] + index_at[longest + 1:]
    return values.at[tuple(index_at)].set(least).at[tuple(next_to)].set(top_value)


def levels(own_key, dims, pieces, low, high):
    def one(dim, shards_of):
        draws = jax.random.uniform(jax.random.fold_in(jax.random.fold_in(own_key, 6), dim), (shards_of,), jnp.float32, low / len(pieces), high / len(pieces))
        return jnp.repeat(jnp.exp(draws), dims[dim] // shards_of).reshape((-1,) + (1,) * (len(dims) - dim - 1))

    gain = one(*pieces[0])
    for cut in pieces[1:]:
        gain = gain * one(*cut)
    return gain


def scatter_about(key, dims, deviation, reach, kind=jnp.bfloat16):
    values = deviation * jax.random.normal(key, dims, jnp.float32)
    return jnp.clip(values, min=-reach, max=reach).astype(kind)


def setup_inputs(seed: int = 0) -> dict:
    streams_of = jax.random.split(jax.random.key(seed), 12)
    saved_paths = draw_saved_paths(jax.random.fold_in(streams_of[11], 71), 0)
    pca_basis = draw_pca_basis(jax.random.fold_in(streams_of[11], 71), 0)
    vol_surface = jnp.clip(jnp.exp(math.log(2.0) - 1.3862944 * jax.random.uniform(streams_of[2], (NT, F), jnp.float32) ** levels(streams_of[2], (NT, F), ((0, 4),), -0.2, 0.2)), 0.5, 2.0)
    chol_factor = draw_chol_factor(jax.random.fold_in(streams_of[11], 71), 0)
    exposure_load = scatter_about(streams_of[4], (NE, F), F ** -0.5, 0.25, jnp.float32)
    reset_load = scatter_about(streams_of[5], (NE, F), (F * NT // NE) ** -0.5, 0.0234375, jnp.float32)
    strikes = scatter_about(streams_of[6], (NE,), 1.0, 4.0, jnp.float32)
    bucket_weight = jnp.clip(jnp.exp(jax.random.uniform(streams_of[7], (NE,), jnp.float32, math.log(0.5), math.log(2.0))), 0.5, 2.0)
    bucket_start = draw_bucket_start(jax.random.fold_in(streams_of[11], 71), 0)
    generator = with_ends(jax.random.randint(streams_of[9], (F,), 1, 1048576), jax.random.fold_in(streams_of[9], 1), 1, 1048575).astype(jnp.int32)
    point_ids = with_ends(jax.random.randint(streams_of[10], (POINTS,), 0, 1048576), jax.random.fold_in(streams_of[10], 1), 0, 1048575).astype(jnp.int32)
    return dict(saved_paths=saved_paths, pca_basis=pca_basis, vol_surface=vol_surface, chol_factor=chol_factor, exposure_load=exposure_load, reset_load=reset_load, strikes=strikes, bucket_weight=bucket_weight, bucket_start=bucket_start, generator=generator, point_ids=point_ids)


def lattice_shift(point_ids, generator):
    gen_low = generator % 1024
    gen_high = generator // 1024
    low_part = (point_ids[:, None] * gen_low[None, :]) % 1048576
    high_part = ((point_ids[:, None] * gen_high[None, :]) % 1024) * 1024
    residue = (low_part + high_part) % 1048576
    uniform_pts = (residue.astype(jnp.float32) + 0.5) / 1048576.0
    return 0.5 * 3.4641016151377544 * (uniform_pts - 0.5)


def reference(saved_paths, pca_basis, vol_surface, chol_factor, exposure_load, reset_load, strikes, bucket_weight, bucket_start, generator, point_ids):
    highest = lax.Precision.HIGHEST
    start_state = lattice_shift(point_ids, generator)
    step_index = jnp.arange(NT, dtype=jnp.int32)
    next_start = jnp.concatenate([bucket_start[1:], jnp.full((1,), NT, jnp.int32)])
    member = ((step_index[:, None] >= bucket_start[None, :]) & (step_index[:, None] < next_start[None, :])).astype(jnp.float32)
    flat_paths = saved_paths.reshape(NT * POINTS, F)
    factor_level = jnp.dot(flat_paths, chol_factor.T, preferred_element_type=jnp.float32).reshape(NT, POINTS, F)
    path_state = start_state[None, :, :] + vol_surface[:, None, :] * factor_level
    reset_state = path_state[bucket_start]
    load_steps = jnp.dot(member, exposure_load, precision=highest)
    reset_term = jnp.sum(reset_load[:, None, :] * reset_state, axis=2)
    margin = jnp.sum(load_steps[:, None, :] * path_state, axis=2) + jnp.dot(member, reset_term, precision=highest) - jnp.dot(member, strikes, precision=highest)[:, None]
    sensitivity = jnp.dot(member, bucket_weight, precision=highest)[:, None] * jax.nn.sigmoid(margin)
    bucket_sens = jnp.dot(member.T, sensitivity, precision=highest)
    adj_state = sensitivity[:, :, None] * load_steps[:, None, :]
    adj_state = adj_state.at[bucket_start].add(bucket_sens[:, :, None] * reset_load[:, None, :])
    vol_greeks = jnp.sum(adj_state * factor_level, axis=1)
    scaled_adj = (vol_surface[:, None, :] * adj_state).astype(jnp.bfloat16)
    flat_scaled = scaled_adj.reshape(NT * POINTS, F)
    chol_greeks = jnp.dot(flat_scaled.T, flat_paths, preferred_element_type=jnp.float32) / NT
    adj_path = jnp.dot(flat_scaled, chol_factor, preferred_element_type=jnp.float32).astype(jnp.bfloat16)
    normal_adjoint = jnp.dot(pca_basis, adj_path.reshape(NT, POINTS * F), preferred_element_type=jnp.float32).reshape(NT, POINTS, F)
    return normal_adjoint, vol_greeks, chol_greeks
```

```python
import jax
import jax.numpy as jnp
from jax import lax
from jax.experimental import pallas as pl
from jax.experimental.pallas import tpu as pltpu
from jax.sharding import Mesh, PartitionSpec as P

BF = jnp.bfloat16
F32 = jnp.float32
ALL = ("yl", "c", "yh", "z", "x")
TM = ("yl", "c")
PTS = ("yh", "z", "x")
BUCKETS = 32
STEPS = 1024
BLOCKS = 4
CHUNK = 256
CHUNKS = STEPS // CHUNK
NF = 512
WROWS = 5 * BUCKETS
VMEM_LIMIT = 48 * 1024 * 1024

NN = (((1,), (0,)), ((), ()))
NT = (((1,), (1,)), ((), ()))
TN = (((0,), (0,)), ((), ()))


def dot(a, b, dims):
    return lax.dot_general(a, b, dims, preferred_element_type=F32)


def split2(x):
    hi = x.astype(BF)
    return hi, (x - hi.astype(F32)).astype(BF)


def one_hots(first_step, count, start, nxt):
    t = first_step + lax.broadcasted_iota(jnp.int32, (BUCKETS, count), 1)
    member = jnp.where((t >= start) & (t < nxt), 1.0, 0.0)
    at_start = jnp.where(t == start, 1.0, 0.0)
    return member, at_start


def margin_kernel(pos, paths, vol, chol, start_state, load, reset, bstart, bnext, out):
    i = pl.program_id(0)
    level = dot(paths[...], chol[...], NT)
    state = start_state[...] + vol[...] * level
    s1, s2 = split2(state)
    l1, l2 = split2(load[...])
    r1, r2 = split2(reset[...])
    big = dot(jnp.concatenate([l1, l2, r1, r2], axis=0), s1, NT)
    small = dot(jnp.concatenate([l1, r1], axis=0), s2, NT)
    n = BUCKETS
    m = big[0:n] + big[n : 2 * n] + small[0:n]
    r = big[2 * n : 3 * n] + big[3 * n : 4 * n] + small[n : 2 * n]
    member, at_start = one_hots(pos[0] * STEPS + i * CHUNK, CHUNK, bstart[...], bnext[...])
    out[0:1, :] = jnp.sum(member * m, axis=0, keepdims=True)
    out[1:2, :] = jnp.sum(at_start * r, axis=0, keepdims=True)


def sens_kernel(
    pos, y, paths, vol, chol, load, reset, strikes, weight, bstart, bnext, wt, bmat, vl, cg, acc
):
    i = pl.program_id(0)

    @pl.when(i == 0)
    def _():
        hots = [one_hots(b * STEPS, STEPS, bstart[...], bnext[...]) for b in range(BLOCKS)]
        l1, l2 = split2(load[...])
        for q in range(2):
            term = sum(
                jnp.sum(hots[b][1] * y[b, q, 1:2, :], axis=1, keepdims=True) for b in range(BLOCKS)
            )
            offset = term - strikes[...]
            total = jnp.zeros((BUCKETS, 1), F32)
            for b in range(BLOCKS):
                member, at_start = hots[b]
                margin = y[b, q, 0:1, :] + jnp.sum(member * offset, axis=0, keepdims=True)
                gain = jnp.sum(member * weight[...], axis=0, keepdims=True)
                ms = member * (gain * jax.nn.sigmoid(margin))
                total = total + jnp.sum(ms, axis=1, keepdims=True)
                m1, m2 = split2(ms)
                a = at_start.astype(BF)
                wt[q, b] = jnp.concatenate([m1, m1, m2, a, a], axis=0)
            r1, r2 = split2(total * reset[...])
            bmat[q] = jnp.concatenate([l1, l2, l1, r1, r2], axis=0)
        acc[...] = jnp.zeros_like(acc)

    lanes = pl.ds(pl.multiple_of(i * CHUNK, CHUNK), CHUNK)
    adj = dot(wt[pos[1], pos[0], :, lanes], bmat[pos[1]], TN)
    level = dot(paths[...], chol[...], NT)
    vl[...] = (adj * level).astype(BF)
    scaled = (vol[...] * adj).astype(BF)
    acc[...] += dot(scaled, paths[...], TN)

    @pl.when(i == CHUNKS - 1)
    def _():
        cg[...] = acc[...].astype(BF)


def adjoint_kernel(pos, basis, v0, v1, v2, v3, wt, bmat, chol, own, other, acc):
    r = pl.program_id(0)
    b = jnp.where(r == 0, pos[2], jnp.where(r == 1, pos[3], jnp.where(r == 2, pos[4], pos[5])))

    @pl.when(r == 0)
    def _():
        acc[...] = jnp.zeros_like(acc)

    for k, v in enumerate((v0, v1, v2, v3)):

        @pl.when(r == k)
        def _(v=v):
            for j in range(CHUNKS):
                rows = pl.ds(j * CHUNK, CHUNK)
                vol = v[rows, :].astype(F32)
                for q in range(2):
                    adj = dot(wt[q, b, :, rows], bmat[q], TN)
                    scaled = (vol * adj).astype(BF)
                    acc[q] += dot(basis[0, :, rows], scaled, NN)

    @pl.when(r == BLOCKS - 1)
    def _():
        for q in range(2):
            h1, h2 = split2(acc[q])
            res = dot(h1, chol[...], NN) + dot(h2, chol[...], NN)

            @pl.when(pos[1] == q)
            def _():
                own[...] = res

            @pl.when(pos[1] != q)
            def _():
                other[...] = res.astype(BF)


def full(shape):
    return pl.BlockSpec(shape, lambda *_: (0,) * len(shape))


SMEM = pl.BlockSpec(memory_space=pltpu.SMEM)
PARAMS = pltpu.CompilerParams(vmem_limit_bytes=VMEM_LIMIT)


def lattice_shift(point_ids, generator):
    gen_low = generator % 1024
    gen_high = generator // 1024
    low_part = point_ids[:, None] * gen_low[None, :] % 1048576
    high_part = point_ids[:, None] * gen_high[None, :] % 1024 * 1024
    residue = (low_part + high_part) % 1048576
    uniform_pts = (residue.astype(F32) + 0.5) / 1048576.0
    return 0.5 * 3.4641016151377544 * (uniform_pts - 0.5)


def flip(axis):
    return [(0, 1), (1, 0)]


def basis_moves():
    moves = []
    for yl in range(2):
        for c in range(2):
            for yh in range(2):
                for z in range(8):
                    for x in range(4):
                        src = (((yl * 2 + c) * 2 + yh) * 8 + z) * 4 + x
                        z2, z1, z0 = z >> 2, (z >> 1) & 1, z & 1
                        to_yl, to_c, to_yh = yh, z2, z1
                        to_z = ((yl ^ to_yl) * 2 + (c ^ to_c)) * 2 + z0
                        moves.append((src, (((to_yl * 2 + to_c) * 2 + to_yh) * 8 + to_z) * 4 + x))
    return moves


def exchange(parts, axis, size):
    return lax.all_to_all(parts, axis, split_axis=0, concat_axis=0, tiled=True)


def gather(x, axis, size):
    return lax.all_to_all(
        jnp.broadcast_to(x[None], (size,) + x.shape), axis, split_axis=0, concat_axis=0, tiled=True
    )


def body(
    saved_paths,
    pca_basis,
    vol_surface,
    chol_factor,
    exposure_load,
    reset_load,
    strikes,
    bucket_weight,
    bucket_start,
    generator,
    point_ids,
):
    yl, c, yh = lax.axis_index("yl"), lax.axis_index("c"), lax.axis_index("yh")
    block = yl * 2 + c
    pos = jnp.stack([block, yh, block, block ^ 1, block ^ 2, block ^ 3]).astype(jnp.int32)
    paths = saved_paths.reshape(STEPS, NF)
    bstart = bucket_start[:, None]
    bnext = jnp.concatenate([bucket_start[1:], jnp.full((1,), BLOCKS * STEPS, jnp.int32)])[:, None]
    start_state = lattice_shift(point_ids, generator)

    moved = lax.ppermute(pca_basis, ALL, basis_moves())
    basis = lax.all_gather(moved, ("z", "x"), axis=0, tiled=True).reshape(BLOCKS, STEPS // 2, STEPS)

    v0 = vol_surface.astype(BF)
    v2 = lax.ppermute(v0, "yl", flip("yl"))
    v1 = lax.ppermute(v0, "c", flip("c"))
    v3 = lax.ppermute(v2, "c", flip("c"))

    rows = pl.BlockSpec((CHUNK, NF), lambda i: (i, 0))
    bucket_rows = full((BUCKETS, NF))
    bucket_col = full((BUCKETS, 1))
    square = full((NF, NF))
    y_own = pl.pallas_call(
        margin_kernel,
        grid=(CHUNKS,),
        in_specs=[SMEM, rows, rows, square, full((1, NF)), bucket_rows, bucket_rows, bucket_col, bucket_col],
        out_specs=pl.BlockSpec((2, CHUNK), lambda i: (0, i)),
        out_shape=jax.ShapeDtypeStruct((2, STEPS), F32),
        compiler_params=PARAMS,
        name="margins",
    )(pos, paths, vol_surface, chol_factor, start_state, exposure_load, reset_load, bstart, bnext)
    y_all = lax.all_gather(y_own, ("yl", "c", "yh"), axis=0).reshape(BLOCKS, 2, 2, STEPS)

    wt, bmat, vol_part, chol_part = pl.pallas_call(
        sens_kernel,
        grid=(CHUNKS,),
        in_specs=[SMEM, full((BLOCKS, 2, 2, STEPS)), rows, rows, square, bucket_rows, bucket_rows]
        + [bucket_col] * 4,
        out_specs=[full((2, BLOCKS, WROWS, STEPS)), full((2, WROWS, NF)), rows, square],
        out_shape=[
            jax.ShapeDtypeStruct((2, BLOCKS, WROWS, STEPS), BF),
            jax.ShapeDtypeStruct((2, WROWS, NF), BF),
            jax.ShapeDtypeStruct((STEPS, NF), BF),
            jax.ShapeDtypeStruct((NF, NF), BF),
        ],
        scratch_shapes=[pltpu.VMEM((NF, NF), F32)],
        compiler_params=PARAMS,
        name="sensitivities",
    )(
        pos, y_all, paths, vol_surface, chol_factor, exposure_load, reset_load,
        strikes[:, None], bucket_weight[:, None], bstart, bnext,
    )

    half = NF // 2
    kept = lax.dynamic_slice_in_dim(chol_part, c * half, half, 0).astype(F32)
    sent = lax.dynamic_slice_in_dim(chol_part, (1 - c) * half, half, 0)
    chol_half = (kept + lax.ppermute(sent, "c", flip("c")).astype(F32)).astype(BF)
    parts = jnp.concatenate([vol_part.reshape(4, 256, NF), chol_half.reshape(4, 64, NF)], axis=1)
    over_x = jnp.sum(exchange(parts, "x", 4).astype(F32), axis=0).astype(BF)
    parts = jnp.concatenate(
        [over_x[:256].reshape(8, 32, NF), over_x[256:].reshape(8, 8, NF)], axis=1
    )
    over_z = jnp.sum(exchange(parts, "z", 8).astype(F32), axis=0)
    parts = jnp.concatenate([over_z[:32].reshape(2, 16, NF), over_z[32:].reshape(2, 4, NF)], axis=1)
    kept = lax.dynamic_index_in_dim(parts, yh, 0, keepdims=False)
    sent = lax.dynamic_index_in_dim(parts, 1 - yh, 0, keepdims=False)
    mine = kept + lax.ppermute(sent, "yh", flip("yh"))
    chol_rows = mine[16:] + lax.ppermute(mine[16:], "yl", flip("yl"))
    mine = jnp.concatenate([mine[:16], chol_rows], axis=0).astype(BF)
    theirs = lax.ppermute(mine, "yh", flip("yh"))
    pair = jnp.where(yh == 0, jnp.stack([mine, theirs]), jnp.stack([theirs, mine]))
    all_z = gather(pair, "z", 8)
    all_x = gather(all_z, "x", 4)
    vol_greeks = all_x[:, :, :, :16].reshape(STEPS, NF).astype(F32)
    chol_mine = all_x[:, :, :, 16:].reshape(half, NF)
    chol_theirs = lax.ppermute(chol_mine, "c", flip("c"))
    chol_greeks = (
        jnp.where(
            c == 0,
            jnp.concatenate([chol_mine, chol_theirs]),
            jnp.concatenate([chol_theirs, chol_mine]),
        ).astype(F32)
        / (BLOCKS * STEPS)
    )

    own, other = pl.pallas_call(
        adjoint_kernel,
        grid=(BLOCKS,),
        in_specs=[SMEM, pl.BlockSpec((1, STEPS // 2, STEPS), lambda i: (i, 0, 0))]
        + [full((STEPS, NF))] * 4
        + [full((2, BLOCKS, WROWS, STEPS)), full((2, WROWS, NF)), square],
        out_specs=[full((STEPS // 2, NF))] * 2,
        out_shape=[
            jax.ShapeDtypeStruct((STEPS // 2, NF), F32),
            jax.ShapeDtypeStruct((STEPS // 2, NF), BF),
        ],
        scratch_shapes=[pltpu.VMEM((2, STEPS // 2, NF), F32)],
        compiler_params=PARAMS,
        name="adjoints",
    )(pos, basis, v0, v1, v2, v3, wt, bmat, chol_factor)
    got = lax.ppermute(other, "yh", flip("yh")).astype(F32)
    normal_adjoint = jnp.where(yh == 0, jnp.stack([own, got]), jnp.stack([got, own]))
    return normal_adjoint.reshape(STEPS, 1, NF), vol_greeks, chol_greeks


def solution(mesh):
    split = Mesh(mesh.devices.reshape(2, 2, 2, 8, 4), ALL)
    return jax.shard_map(
        body,
        mesh=split,
        in_specs=(
            P(TM, PTS, None),
            P(PTS, TM),
            P(TM, None),
            P(),
            P(),
            P(),
            P(),
            P(),
            P(),
            P(),
            P(PTS),
        ),
        out_specs=(P(TM, PTS, None), P(TM, None), P()),
        check_vma=False,
    )
```

```python
import jax
import jax.numpy as jnp
from jax import lax
from jax.experimental import pallas as pl
from jax.experimental.pallas import tpu as pltpu
from jax.sharding import Mesh, PartitionSpec as P

BF = jnp.bfloat16
F32 = jnp.float32
I32 = jnp.int32
ALL = ("yl", "c", "yh", "z", "x")
TM = ("yl", "c")
PTS = ("yh", "z", "x")
NB = 32
STEPS = 1024
BLOCKS = 4
CHUNK = 256
NF = 512
GROUP = 4
ROWS = STEPS // GROUP
WROWS = 5 * NB
MIB = 1024 * 1024

NN = (((1,), (0,)), ((), ()))
NT = (((1,), (1,)), ((), ()))
TN = (((0,), (0,)), ((), ()))


def dot(a, b, dims):
    return lax.dot_general(a, b, dims, preferred_element_type=F32)


def split2(x):
    hi = x.astype(BF)
    return hi, (x - hi.astype(F32)).astype(BF)


def column(row, shift=0):
    i = lax.broadcasted_iota(I32, (NB, NB), 0)
    j = lax.broadcasted_iota(I32, (NB, NB), 1)
    return jnp.sum(jnp.where(j == i + shift, row, 0), axis=1, keepdims=True)


def bucket_ends(bstart):
    start = column(bstart)
    last = lax.broadcasted_iota(I32, (NB, 1), 0) == NB - 1
    return start, jnp.where(last, BLOCKS * STEPS, column(bstart, 1))


def one_hots(first_step, count, start, nxt):
    t = first_step + lax.broadcasted_iota(I32, (NB, count), 1)
    member = jnp.where((t >= start) & (t < nxt), 1.0, 0.0)
    at_start = jnp.where(t == start, 1.0, 0.0)
    return member, at_start


def own_block():
    return lax.axis_index("yl") * 2 + lax.axis_index("c")


def margin_kernel(pid, paths, vol, chol, gen, load, reset, bstart, out):
    i = pl.program_id(0)
    low = (pid[0] * (gen[...] & 1023)) & 1048575
    high = ((pid[0] * (gen[...] >> 10)) & 1023) << 10
    residue = (low + high) & 1048575
    start_state = 0.5 * 3.4641016151377544 * ((residue.astype(F32) + 0.5) / 1048576.0 - 0.5)
    state = start_state + vol[...] * dot(paths[...], chol[...], NT)
    s1, s2 = split2(state)
    l1, l2 = split2(load[...])
    r1, r2 = split2(reset[...])
    big = dot(jnp.concatenate([l1, l2, r1, r2], axis=0), s1, NT)
    small = dot(jnp.concatenate([l1, r1], axis=0), s2, NT)
    m = big[0:NB] + big[NB : 2 * NB] + small[0:NB]
    r = big[2 * NB : 3 * NB] + big[3 * NB :] + small[NB:]
    start, nxt = bucket_ends(bstart[...])
    member, at_start = one_hots(own_block() * STEPS + i * CHUNK, CHUNK, start, nxt)
    out[0:1, :] = jnp.sum(member * m, axis=0, keepdims=True)
    out[1:2, :] = jnp.sum(at_start * r, axis=0, keepdims=True)


def bucket_values(y, load, reset, strikes, weight, start, nxt):
    hots = [one_hots(b * STEPS, STEPS, start, nxt) for b in range(BLOCKS)]
    term = sum(jnp.sum(hots[b][1] * y(b)[1:2], axis=1, keepdims=True) for b in range(BLOCKS))
    offset = term - strikes
    total = jnp.zeros((NB, 1), F32)
    rows = []
    for b in range(BLOCKS):
        ms = step_sens(y(b), hots[b][0], offset, weight)
        total = total + jnp.sum(ms, axis=1, keepdims=True)
        rows.append((ms, hots[b][1]))
    l1, l2 = split2(load)
    r1, r2 = split2(total * reset)
    return rows, offset, jnp.concatenate([l1, l2, l1, r1, r2], axis=0)


def step_sens(y, member, offset, weight):
    margin = y[0:1] + jnp.sum(member * offset, axis=0, keepdims=True)
    gain = jnp.sum(member * weight, axis=0, keepdims=True)
    return member * (gain * jax.nn.sigmoid(margin))


def hot_rows(ms, at_start):
    m1, m2 = split2(ms)
    a = at_start.astype(BF)
    return jnp.concatenate([m1, m1, m2, a, a], axis=0)


def sens_kernel(
    y, paths, vol, chol, load, reset, strikes, weight, bstart, kept, o1, o2, o3, wt, bmat
):
    i = pl.program_id(0)

    @pl.when(i == 0)
    def _():
        start, nxt = bucket_ends(bstart[...])
        w = column(weight[...])
        _, offset, factors = bucket_values(
            lambda b: y[b], load[...], reset[...], column(strikes[...]), w, start, nxt
        )
        own = own_block()
        member, at_start = one_hots(own * STEPS, STEPS, start, nxt)
        wt[...] = hot_rows(step_sens(y[own], member, offset, w), at_start)
        bmat[...] = factors

    at = pl.ds(pl.multiple_of(lax.rem(lax.axis_index("x") + i, 4) * CHUNK, CHUNK), CHUNK)
    adj = dot(wt[:, at], bmat[...], TN)
    term = adj * dot(paths[at, :], chol[...], NT)

    @pl.when(i == 0)
    def _():
        kept[...] = term

    for k, o in enumerate((o1, o2, o3)):

        @pl.when(i == k + 1)
        def _(o=o):
            o[...] = term.astype(BF)


def chol_kernel(wt, bmat, paths, vol, kept, sent, acc):
    i = pl.program_id(0)
    at = pl.ds(pl.multiple_of(i * CHUNK, CHUNK), CHUNK)
    scaled = (vol[...] * dot(wt[:, at], bmat[...], TN)).astype(BF)
    new = dot(scaled, paths[...], TN)

    @pl.when(i == 0)
    def _():
        acc[...] = new

    @pl.when(i > 0)
    def _():
        acc[...] += new

    @pl.when(i == STEPS // CHUNK - 1)
    def _():
        half = NF // 2
        c = lax.axis_index("c")
        kept[...] = acc[pl.ds(pl.multiple_of(c * half, half), half), :]
        sent[...] = acc[pl.ds(pl.multiple_of((1 - c) * half, half), half), :]


def chol_pieces_kernel(kept, got, k, o1, o2, o3):
    x = lax.axis_index("x")
    rows = NF // 8
    for d, o in enumerate((k, o1, o2, o3)):
        at = pl.ds(pl.multiple_of(lax.rem(x + d, 4) * rows, rows), rows)
        o[...] = (kept[at, :] + got[at, :]).astype(o.dtype)


def sum_x_kernel(v0, v1, v2, v3, c0, c1, c2, c3, *outs):
    *pieces, vsum, csum = outs
    vsum[...] = v0[...] + v1[...].astype(F32) + v2[...].astype(F32) + v3[...].astype(F32)
    csum[...] = c0[...] + c1[...].astype(F32) + c2[...].astype(F32) + c3[...].astype(F32)
    z = lax.axis_index("z")
    zeros = jnp.zeros((8, NF), F32)
    for d, o in enumerate(pieces):
        s = lax.rem(z + d, 8)
        v = vsum[pl.ds(pl.multiple_of(s * 32, 32), 32), :]
        c = csum[pl.ds(pl.multiple_of(s * 8, 8), 8), :]
        o[...] = jnp.concatenate([v, c, zeros], axis=0).astype(o.dtype)


def sum_z_kernel(k, g1, g2, g3, g4, g5, g6, g7, out, chol_out):
    total = k[...]
    for g in (g1, g2, g3, g4, g5, g6, g7):
        total = total + g[...].astype(F32)
    out[...] = total
    chol_out[...] = total[32:40]


def pair_kernel(own, got, c_yl, c_both, out):
    total = own[...] + got[...]
    extra = c_yl[...] + c_both[...]
    out[...] = jnp.concatenate([total[:32], total[32:40] + extra, total[40:]], axis=0).astype(BF)


def spread_z_kernel(k, g1, g2, g3, g4, g5, g6, g7, vol_out, chol_out, vtmp, ctmp):
    z = lax.axis_index("z")
    for d, g in enumerate((k, g1, g2, g3, g4, g5, g6, g7)):
        s = lax.rem(z + 8 - d, 8)
        rows = g[...].astype(F32)
        vtmp[pl.ds(pl.multiple_of(s * 32, 32), 32), :] = rows[:32]
        ctmp[pl.ds(pl.multiple_of(s * 8, 8), 8), :] = rows[32:40]
    vol_out[...] = vtmp[...].astype(BF)
    chol_out[...] = ctmp[...].astype(BF)


def vol_out_kernel(k, g1, g2, g3, out):
    x = lax.axis_index("x")
    for d, g in enumerate((k, g1, g2, g3)):
        at = pl.ds(pl.multiple_of(lax.rem(x + 4 - d, 4) * 256, 256), 256)
        out[at, :] = g[...].astype(F32)


def chol_half_kernel(k, g1, g2, g3, out, tmp):
    x = lax.axis_index("x")
    for d, g in enumerate((k, g1, g2, g3)):
        tmp[pl.ds(pl.multiple_of(lax.rem(x + 4 - d, 4) * 64, 64), 64), :] = g[...].astype(F32)
    out[...] = tmp[...].astype(BF)


def chol_out_kernel(own, got, out):
    c = lax.axis_index("c")
    scale = 1.0 / (BLOCKS * STEPS)
    out[pl.ds(pl.multiple_of(c * 256, 256), 256), :] = own[...].astype(F32) * scale
    out[pl.ds(pl.multiple_of((1 - c) * 256, 256), 256), :] = got[...].astype(F32) * scale


def scaled_kernel(
    y0, y1, y2, y3, v0, v1, v2, v3, load, reset, strikes, weight, bstart, out, wt, bmat
):
    r = pl.program_id(0)

    @pl.when(r == 0)
    def _():
        start, nxt = bucket_ends(bstart[...])
        w, k = column(weight[...]), column(strikes[...])
        for q, y in enumerate((y0, y1, y2, y3)):
            rows, _, factors = bucket_values(lambda b: y[b], load[...], reset[...], k, w, start, nxt)
            for b in range(BLOCKS):
                wt[q, b] = hot_rows(*rows[b])
            bmat[q] = factors

    b = own_block() ^ r
    for k, v in enumerate((v0, v1, v2, v3)):

        @pl.when(r == k)
        def _(v=v):
            for j in range(STEPS // CHUNK):
                rows = slice(j * CHUNK, (j + 1) * CHUNK)
                vol = v[rows, :].astype(F32)
                for q in range(GROUP):
                    adj = dot(wt[q, b, :, rows], bmat[q], TN)
                    out[0, rows, q * NF : (q + 1) * NF] = (vol * adj).astype(BF)


def adjoint_kernel(basis, scaled, chol, own, o1, o2, o3, acc):
    r = pl.program_id(0)
    new = dot(basis[0], scaled[0], NN)

    @pl.when(r == 0)
    def _():
        acc[...] = new

    @pl.when(r > 0)
    def _():
        acc[...] += new

    @pl.when(r == BLOCKS - 1)
    def _():
        for q, o in enumerate((own, o1, o2, o3)):
            h1, h2 = split2(acc[:, q * NF : (q + 1) * NF])
            o[...] = (dot(h1, chol[...], NN) + dot(h2, chol[...], NN)).astype(o.dtype)


def normals_kernel(own, g1, g2, g3, out):
    mine = lax.axis_index("yh") * 2 + (lax.axis_index("x") & 1)
    for q, g in enumerate((own, g1, g2, g3)):
        first = pl.multiple_of((mine ^ q) * (ROWS * 4), ROWS * 4)
        for j in range(4):
            at = pl.ds(first + j, ROWS, stride=4)
            out[at, :] = g[:, j * 128 : (j + 1) * 128].astype(F32)


def full(shape):
    return pl.BlockSpec(shape, lambda *_: (0,) * len(shape))


def call(kernel, args, outs, name, vmem=40, scratch=(), **kw):
    single = len(outs) == 1
    shapes = [jax.ShapeDtypeStruct(s, d) for s, d in outs]
    spec = dict(
        in_specs=[full(a.shape) for a in args], out_specs=[full(s.shape) for s in shapes], grid=(1,)
    )
    spec.update(kw)
    if single and isinstance(spec["out_specs"], list):
        spec["out_specs"] = spec["out_specs"][0]
    return pl.pallas_call(
        kernel,
        out_shape=shapes[0] if single else shapes,
        scratch_shapes=list(scratch),
        compiler_params=pltpu.CompilerParams(vmem_limit_bytes=vmem * MIB),
        name=name,
        **spec,
    )(*args)


def basis_moves():
    moves = []
    for yl in range(2):
        for c in range(2):
            for yh in range(2):
                for z in range(8):
                    for x in range(4):
                        src = (((yl * 2 + c) * 2 + yh) * 8 + z) * 4 + x
                        z2, z1, z0 = z >> 2, (z >> 1) & 1, z & 1
                        to_z = (((yl ^ yh) * 2 + (c ^ z2)) * 2) + (x >> 1)
                        to_x = (x & 1) * 2 + z0
                        moves.append((src, (((yh * 2 + z2) * 2 + z1) * 8 + to_z) * 4 + to_x))
    return moves


def swap(x, axis):
    return lax.ppermute(x, axis, [(0, 1), (1, 0)])


def shift(x, axis, size, d):
    return lax.ppermute(x, axis, [(i, (i + d) % size) for i in range(size)])


def swap_x(x, bit):
    return lax.ppermute(x, "x", [(i, i ^ bit) for i in range(4)])


def body(
    saved_paths,
    pca_basis,
    vol_surface,
    chol_factor,
    exposure_load,
    reset_load,
    strikes,
    bucket_weight,
    bucket_start,
    generator,
    point_ids,
):
    paths = saved_paths.reshape(STEPS, NF)
    bstart = bucket_start.reshape(1, NB)
    strike_row = strikes.reshape(1, NB)
    weight_row = bucket_weight.reshape(1, NB)

    moved = lax.ppermute(pca_basis, ALL, basis_moves())
    across = swap_x(moved, 2)
    high = lax.axis_index("x") >> 1
    pair = jnp.where(high == 0, jnp.stack([moved, across]), jnp.stack([across, moved]))
    basis = lax.all_gather(pair, "z", axis=0, tiled=True).reshape(BLOCKS, ROWS, STEPS)

    row_spec = pl.BlockSpec((CHUNK, NF), lambda i: (i, 0))
    square = full((NF, NF))
    bucket_rows = full((NB, NF))
    bucket_row = full((1, NB))
    y_own = call(
        margin_kernel,
        (
            point_ids, paths, vol_surface, chol_factor, generator.reshape(1, NF), exposure_load,
            reset_load, bstart,
        ),
        [((2, STEPS), F32)],
        "margins",
        vmem=60,
        grid=(STEPS // CHUNK,),
        in_specs=[
            pl.BlockSpec(memory_space=pltpu.SMEM), row_spec, row_spec, square, full((1, NF)),
            bucket_rows, bucket_rows, bucket_row,
        ],
        out_specs=pl.BlockSpec((2, CHUNK), lambda i: (0, i)),
    )
    y0 = lax.all_gather(y_own, TM, axis=0)

    kept, v1, v2, v3, wt, bmat = call(
        sens_kernel,
        (
            y0, paths, vol_surface, chol_factor, exposure_load, reset_load, strike_row, weight_row,
            bstart,
        ),
        [((CHUNK, NF), F32)] + [((CHUNK, NF), BF)] * 3 + [((WROWS, STEPS), BF), ((WROWS, NF), BF)],
        "sensitivities",
        grid=(4,),
    )
    v1, v2, v3 = (shift(v, "x", 4, d + 1) for d, v in enumerate((v1, v2, v3)))

    ck, cs = call(
        chol_kernel,
        (wt, bmat, paths, vol_surface),
        [((NF // 2, NF), F32)] * 2,
        "chol_term",
        grid=(STEPS // CHUNK,),
        in_specs=[full((WROWS, STEPS)), full((WROWS, NF)), row_spec, row_spec],
        scratch=[pltpu.VMEM((NF, NF), F32)],
    )
    c0, c1, c2, c3 = call(
        chol_pieces_kernel,
        (ck, swap(cs, "c")),
        [((64, NF), F32)] + [((64, NF), BF)] * 3,
        "chol_pieces",
    )
    c1, c2, c3 = (shift(v, "x", 4, d + 1) for d, v in enumerate((c1, c2, c3)))

    pieces = call(
        sum_x_kernel,
        (kept, v1, v2, v3, c0, c1, c2, c3),
        [((48, NF), F32)] + [((48, NF), BF)] * 7,
        "sum_x",
        scratch=[pltpu.VMEM((CHUNK, NF), F32), pltpu.VMEM((64, NF), F32)],
    )
    pieces = [pieces[0]] + [shift(p, "z", 8, d + 1) for d, p in enumerate(pieces[1:])]
    part, cpart = call(sum_z_kernel, pieces, [((48, NF), F32), ((8, NF), F32)], "sum_z")
    other_y = [(a * 2 + b, (1 - a) * 2 + 1 - b) for a in range(2) for b in range(2)]
    total = call(
        pair_kernel,
        (part, swap(part, "yh"), swap(cpart, "yl"), lax.ppermute(cpart, ("yl", "yh"), other_y)),
        [((48, NF), BF)],
        "totals",
    )
    spread = [total] + [shift(total, "z", 8, d) for d in range(1, 8)]
    vol_z, chol_z = call(
        spread_z_kernel,
        spread,
        [((CHUNK, NF), BF), ((64, NF), BF)],
        "spread_z",
        scratch=[pltpu.VMEM((CHUNK, NF), F32), pltpu.VMEM((64, NF), F32)],
    )
    vol_x = [vol_z] + [shift(vol_z, "x", 4, d) for d in range(1, 4)]
    vol_greeks = call(vol_out_kernel, vol_x, [((STEPS, NF), F32)], "vol_out")
    chol_x = [chol_z] + [shift(chol_z, "x", 4, d) for d in range(1, 4)]
    chol_half = call(
        chol_half_kernel,
        chol_x,
        [((NF // 2, NF), BF)],
        "chol_half",
        scratch=[pltpu.VMEM((NF // 2, NF), F32)],
    )
    chol_greeks = call(
        chol_out_kernel, (chol_half, swap(chol_half, "c")), [((NF, NF), F32)], "chol_out"
    )

    y1 = swap_x(y0, 1)
    y2 = swap(y0, "yh")
    both = [(a * 4 + b, (1 - a) * 4 + (b ^ 1)) for a in range(2) for b in range(4)]
    y3 = lax.ppermute(y0, ("yh", "x"), both)
    s1 = swap(vol_surface, "c")
    s2 = swap(vol_surface.astype(BF), "yl")
    s3 = swap(s2, "c")
    args = (
        y0, y1, y2, y3, vol_surface, s1, s2, s3, exposure_load, reset_load, strike_row, weight_row,
        bstart,
    )
    scaled = call(
        scaled_kernel,
        args,
        [((BLOCKS, STEPS, GROUP * NF), BF)],
        "scaled",
        grid=(BLOCKS,),
        out_specs=pl.BlockSpec((1, STEPS, GROUP * NF), lambda r: (r, 0, 0)),
        scratch=[
            pltpu.VMEM((GROUP, BLOCKS, WROWS, STEPS), BF),
            pltpu.VMEM((GROUP, WROWS, NF), BF),
        ],
    )
    own, o1, o2, o3 = call(
        adjoint_kernel,
        (basis, scaled, chol_factor),
        [((ROWS, NF), F32)] + [((ROWS, NF), BF)] * 3,
        "adjoints",
        grid=(BLOCKS,),
        in_specs=[
            pl.BlockSpec((1, ROWS, STEPS), lambda r: (r, 0, 0)),
            pl.BlockSpec((1, STEPS, GROUP * NF), lambda r: (r, 0, 0)),
            square,
        ],
        scratch=[pltpu.VMEM((ROWS, GROUP * NF), F32)],
    )
    normals = call(
        normals_kernel,
        (own, swap_x(o1, 1), swap(o2, "yh"), lax.ppermute(o3, ("yh", "x"), both)),
        [((STEPS * 4, 128), F32)],
        "normals",
    )
    return normals.reshape(STEPS, 1, NF), vol_greeks, chol_greeks


def solution(mesh):
    split = Mesh(mesh.devices.reshape(2, 2, 2, 8, 4), ALL)
    return jax.shard_map(
        body,
        mesh=split,
        in_specs=(
            P(TM, PTS, None),
            P(PTS, TM),
            P(TM, None),
            P(),
            P(),
            P(),
            P(),
            P(),
            P(),
            P(),
            P(PTS),
        ),
        out_specs=(P(TM, PTS, None), P(TM, None), P()),
        check_vma=False,
    )
```

```python
import jax
import jax.numpy as jnp
from jax import lax
from jax.experimental import pallas as pl
from jax.experimental.pallas import tpu as pltpu
from jax.sharding import Mesh, PartitionSpec as P

BF = jnp.bfloat16
F32 = jnp.float32
I32 = jnp.int32
ALL = ("yl", "c", "yh", "z", "x1", "x0")
TM = ("yl", "c")
X = ("x1", "x0")
PTS = ("yh", "z", "x1", "x0")
PEERS = ("yh", "x0")
NB = 32
STEPS = 1024
BLOCKS = 4
CHUNK = 256
NF = 512
GROUP = 4
ROWS = STEPS // GROUP
WROWS = 5 * NB
MIB = 1024 * 1024

NN = (((1,), (0,)), ((), ()))
NT = (((1,), (1,)), ((), ()))
TN = (((0,), (0,)), ((), ()))


def dot(a, b, dims):
    return lax.dot_general(a, b, dims, preferred_element_type=F32)


def split2(x):
    hi = x.astype(BF)
    return hi, (x - hi.astype(F32)).astype(BF)


def split3(x):
    hi, mid = split2(x)
    return hi, mid, (x - hi.astype(F32) - mid.astype(F32)).astype(BF)


def column(row, shift=0):
    i = lax.broadcasted_iota(I32, (NB, NB), 0)
    j = lax.broadcasted_iota(I32, (NB, NB), 1)
    return jnp.sum(jnp.where(j == i + shift, row, 0), axis=1, keepdims=True)


def bucket_ends(bstart):
    start = column(bstart)
    last = lax.broadcasted_iota(I32, (NB, 1), 0) == NB - 1
    return start, jnp.where(last, BLOCKS * STEPS, column(bstart, 1))


def bucket_rows(bstart):
    i = lax.broadcasted_iota(I32, (NB, NB), 0)
    j = lax.broadcasted_iota(I32, (NB, NB), 1)
    nxt = jnp.sum(jnp.where(i == j + 1, column(bstart), 0), axis=0, keepdims=True)
    last = lax.broadcasted_iota(I32, (1, NB), 1) == NB - 1
    nxt = jnp.where(last, BLOCKS * STEPS, nxt)
    return jnp.concatenate([bstart] * 4, axis=1), jnp.concatenate([nxt] * 4, axis=1)


def one_hots(first_step, count, start, nxt):
    t = first_step + lax.broadcasted_iota(I32, (NB, count), 1)
    member = jnp.where((t >= start) & (t < nxt), 1.0, 0.0)
    at_start = jnp.where(t == start, 1.0, 0.0)
    return member, at_start


def own_block():
    return lax.axis_index("yl") * 2 + lax.axis_index("c")


def margin_kernel(pid, paths, vol, chol, gen, load, reset, bstart, out):
    i = pl.program_id(0)
    low = (pid[0] * (gen[...] & 1023)) & 1048575
    high = ((pid[0] * (gen[...] >> 10)) & 1023) << 10
    residue = (low + high) & 1048575
    start_state = 0.5 * 3.4641016151377544 * ((residue.astype(F32) + 0.5) / 1048576.0 - 0.5)
    state = start_state + vol[...] * dot(paths[...], chol[...], NT)
    s1, s2 = split2(state)
    l1, l2 = split2(load[...])
    r1, r2 = split2(reset[...])
    none = jnp.zeros_like(l1)
    by_bucket = dot(s1, jnp.concatenate([l1, l2, r1, r2], axis=0), NT) + dot(
        s2, jnp.concatenate([l1, none, r1, none], axis=0), NT
    )
    start, nxt = bucket_rows(bstart[...])
    t = own_block() * STEPS + i * CHUNK + lax.broadcasted_iota(I32, (CHUNK, 4 * NB), 0)
    lane = lax.broadcasted_iota(I32, (CHUNK, 4 * NB), 1)
    margin = jnp.where((lane < 2 * NB) & (t >= start) & (t < nxt), by_bucket, 0.0)
    term = jnp.where((lane >= 2 * NB) & (t == start), by_bucket, 0.0)
    margin = jnp.sum(margin, axis=1, keepdims=True)
    term = jnp.sum(term, axis=1, keepdims=True)
    both = jnp.where(lane == 0, margin, jnp.where(lane == 1, term, 0.0))
    out[...] = jnp.transpose(both)[0:2]


def group_index():
    return lax.axis_index("yh") * 2 + lax.axis_index("x0")


def bucket_values(y, hots, strikes, weight):
    term = sum(jnp.sum(hots[b][1] * y(b)[1:2], axis=1, keepdims=True) for b in range(BLOCKS))
    offset = term - strikes
    total = jnp.zeros((NB, 1), F32)
    rows = []
    for b in range(BLOCKS):
        row = step_sens(y(b), hots[b][0], offset, weight)
        total = total + jnp.sum(hots[b][0] * row, axis=1, keepdims=True)
        rows.append(row)
    return rows, total, offset


def step_sens(y, member, offset, weight):
    margin = y[0:1] + jnp.sum(member * offset, axis=0, keepdims=True)
    gain = jnp.sum(member * weight, axis=0, keepdims=True)
    return gain * jax.nn.sigmoid(margin)


def all_hots(start, nxt):
    return [one_hots(b * STEPS, STEPS, start, nxt) for b in range(BLOCKS)]


def x_index():
    return lax.axis_index("x1") * 2 + lax.axis_index("x0")


def sens_kernel(
    y, paths, vol, chol, load, reset, strikes, weight, bstart, kept, o1, o2, o3, wt, bmat
):
    i = pl.program_id(0)

    @pl.when(i == 0)
    def _():
        start, nxt = bucket_ends(bstart[...])
        w = column(weight[...])
        own = own_block()
        _, total, offset = bucket_values(
            lambda b: y[b], all_hots(start, nxt), column(strikes[...]), w
        )
        member, at_start = one_hots(own * STEPS, STEPS, start, nxt)
        m1, m2 = split2(member * step_sens(y[own], member, offset, w))
        a = at_start.astype(BF)
        wt[...] = jnp.concatenate([m1, m1, m2, a, a], axis=0)
        l1, l2 = split2(load[...])
        r1, r2 = split2(total * reset[...])
        bmat[...] = jnp.concatenate([l1, l2, l1, r1, r2], axis=0)

    at = pl.ds(pl.multiple_of(lax.rem(x_index() + i, 4) * CHUNK, CHUNK), CHUNK)
    term = dot(wt[:, at], bmat[...], TN) * dot(paths[at, :], chol[...], NT)

    @pl.when(i == 0)
    def _():
        kept[...] = term

    for k, o in enumerate((o1, o2, o3)):

        @pl.when(i == k + 1)
        def _(o=o):
            o[...] = term.astype(BF)


def chol_kernel(wt, bmat, paths, vol, kept, sent, acc):
    i = pl.program_id(0)
    at = pl.ds(pl.multiple_of(i * CHUNK, CHUNK), CHUNK)
    scaled = (vol[...] * dot(wt[:, at], bmat[...], TN)).astype(BF)
    new = dot(scaled, paths[...], TN)

    @pl.when(i == 0)
    def _():
        acc[...] = new

    @pl.when(i > 0)
    def _():
        acc[...] += new

    @pl.when(i == STEPS // CHUNK - 1)
    def _():
        c = lax.axis_index("c")
        kept[...] = acc[pl.ds(pl.multiple_of(c * 256, 256), 256), :]
        sent[...] = acc[pl.ds(pl.multiple_of((1 - c) * 256, 256), 256), :]


def chol_split_kernel(own, got, kept, sent):
    yl = lax.axis_index("yl")
    for o, at in ((kept, yl), (sent, 1 - yl)):
        rows = pl.ds(pl.multiple_of(at * 128, 128), 128)
        o[...] = own[rows, :] + got[rows, :]


def sum_x_kernel(kept, g1, g2, g3, c0, c1, out):
    for z in range(8):
        rows = slice(z * 32, z * 32 + 32)
        v = kept[rows, :] + g1[rows, :].astype(F32) + g2[rows, :].astype(F32)
        v = v + g3[rows, :].astype(F32)
        rows = slice(z * 16, z * 16 + 16)
        out[z] = jnp.concatenate([v, c0[rows, :] + c1[rows, :]], axis=0).astype(BF)


def sum_z_kernel(parts, out):
    total = parts[0].astype(F32)
    for k in range(1, parts.shape[0]):
        total = total + parts[k].astype(F32)
    out[...] = total


def total_kernel(own, got, out):
    total = (own[...] + got[...]).astype(BF)
    for z in range(8):
        out[z] = total


def gather_z_kernel(parts, out):
    for z in range(8):
        out[z * 32 : z * 32 + 32, :] = parts[z, 0:32]
        out[256 + z * 16 : 272 + z * 16, :] = parts[z, 32:48]


def greeks_kernel(own, g1, g2, g3, vol_out, chol_out):
    chol = jnp.zeros((128, NF), F32)
    for d, g in enumerate((own, g1, g2, g3)):
        at = pl.ds(pl.multiple_of(lax.rem(x_index() + 4 - d, 4) * 256, 256), 256)
        vol_out[at, :] = g[0:256, :].astype(F32)
        chol = chol + g[256:384, :].astype(F32)
    chol_out[...] = chol.astype(BF)


def chol_half_kernel(own, got, out):
    yl = lax.axis_index("yl")
    for g, at in ((own, yl), (got, 1 - yl)):
        out[pl.ds(pl.multiple_of(at * 128, 128), 128), :] = g[...]


def chol_out_kernel(own, got, out):
    c = lax.axis_index("c")
    for g, at in ((own, c), (got, 1 - c)):
        out[pl.ds(pl.multiple_of(at * 256, 256), 256), :] = g[...].astype(F32) / (BLOCKS * STEPS)


def points_kernel(y, reset, strikes, weight, bstart, cols, radj):
    start, nxt = bucket_ends(bstart[...])
    hots = all_hots(start, nxt)
    w, k = column(weight[...]), column(strikes[...])
    rows = [[] for _ in range(BLOCKS)]
    for q in range(GROUP):
        g = group_index() ^ q
        sens, total, _ = bucket_values(lambda b: y[g, b], hots, k, w)
        radj[q] = total * reset[...]
        for b in range(BLOCKS):
            rows[b].append(sens[b])
    for b in range(BLOCKS):
        cols[b] = jnp.transpose(jnp.concatenate(rows[b] + rows[b], axis=0))


def adjoint_kernel(
    basis_hbm, vol_hbm, s1a, s1b, s2a, s2b, s3a, s3b, cols, radj, chol, load, bstart,
    own, o1, o2, o3, scaled, acc, basis, vol, vols, sems,
):
    half = STEPS // 2
    copies = [[pltpu.make_async_copy(vol_hbm, vol, sems.at[0])]]
    for r, pair in enumerate(((s1a, s1b), (s2a, s2b), (s3a, s3b))):
        copies.append(
            [
                pltpu.make_async_copy(p, vols.at[r, pl.ds(h * half, half)], sems.at[1 + 2 * r + h])
                for h, p in enumerate(pair)
            ]
        )
    for r in range(BLOCKS):
        source = basis_hbm.at[r & 1, r >> 1]
        copies[r].append(pltpu.make_async_copy(source, basis.at[r], sems.at[7 + r]))
        for copy in copies[r]:
            copy.start()
    start, nxt = bucket_ends(bstart[...])
    load_parts = jnp.concatenate(split3(load[...]), axis=0)
    at_resets = jnp.zeros((ROWS, NB), F32)
    vol_resets = jnp.zeros((NB, NF), F32)
    for r in range(BLOCKS):
        for copy in copies[r]:
            copy.wait()
        b = own_block() ^ r
        member, at_start = one_hots(b * STEPS, STEPS, start, nxt)
        member, at_start = member.astype(BF), at_start.astype(BF)
        for j in range(STEPS // CHUNK):
            rows = slice(j * CHUNK, (j + 1) * CHUNK)
            v = vols[r - 1, rows, :] if r else vol[rows, :]
            hot = member[:, rows]
            loads = dot(jnp.concatenate([hot, hot, hot], axis=0), load_parts, TN)
            vol_load = v.astype(F32) * loads
            for q in range(GROUP):
                part = vol_load * cols[b, rows, q : q + 1]
                scaled[r % 2, rows, q * NF : (q + 1) * NF] = part.astype(BF)
            for h in (v,) if r else split2(v):
                vol_resets = vol_resets + dot(at_start[:, rows], h, NN)
        lhs = jnp.concatenate([basis[r, x & 1, x >> 1] for x in range(4)], axis=0)
        new = dot(lhs, scaled[r % 2], NN)
        acc[...] = new if r == 0 else acc[...] + new
        at_resets = at_resets + dot(lhs, at_start, NT)
    at_resets = at_resets.astype(BF)
    for q, o in enumerate((own, o1, o2, o3)):
        more = dot(at_resets, (vol_resets * radj[q]).astype(BF), NN)
        h1, h2 = split2(acc[:, q * NF : (q + 1) * NF] + more)
        o[...] = (dot(h1, chol[...], NN) + dot(h2, chol[...], NN)).astype(o.dtype)


def normals_kernel(own, g1, g2, g3, out):
    for q, g in enumerate((own, g1, g2, g3)):
        first = pl.multiple_of((group_index() ^ q) * (ROWS * 4), ROWS * 4)
        for j in range(4):
            at = pl.ds(first + j, ROWS, stride=4)
            out[at, :] = g[:, j * 128 : (j + 1) * 128].astype(F32)


def full(shape):
    return pl.BlockSpec(shape, lambda *_: (0,) * len(shape))


def call(kernel, args, outs, name, cost, vmem=40, scratch=(), **kw):
    single = len(outs) == 1
    shapes = [jax.ShapeDtypeStruct(s, d) for s, d in outs]
    spec = dict(
        in_specs=[full(a.shape) for a in args], out_specs=[full(s.shape) for s in shapes], grid=(1,)
    )
    spec.update(kw)
    if single and isinstance(spec["out_specs"], list):
        spec["out_specs"] = spec["out_specs"][0]
    return pl.pallas_call(
        kernel,
        out_shape=shapes[0] if single else shapes,
        scratch_shapes=list(scratch),
        cost_estimate=pl.CostEstimate(flops=cost[0], bytes_accessed=cost[1], transcendentals=0),
        compiler_params=pltpu.CompilerParams(vmem_limit_bytes=vmem * MIB),
        name=name,
        **spec,
    )(*args)


def basis_moves(d):
    moves = []
    for yl in range(2):
        for c in range(2):
            for yh in range(2):
                for z in range(8):
                    for x in range(4):
                        src = (((yl * 2 + c) * 2 + yh) * 8 + z) * 4 + x
                        z2, z1, z0 = z >> 2, (z >> 1) & 1, z & 1
                        to_z = (c ^ z2) * 4 + (yl ^ yh) * 2 + (x & 1)
                        to_x = ((x >> 1) ^ d) * 2 + z0
                        moves.append((src, (((yh * 2 + z2) * 2 + z1) * 8 + to_z) * 4 + to_x))
    return moves


def swap(x, axis):
    return lax.ppermute(x, axis, [(0, 1), (1, 0)])


def shift_x(x, d):
    return lax.ppermute(x, X, [(i, (i + d) % 4) for i in range(4)])


def exchange(x, axes):
    return lax.all_to_all(x, axes, split_axis=0, concat_axis=0, tiled=True)


def after(x, *first):
    return lax.optimization_barrier((x,) + first)[0]


def body(
    saved_paths,
    pca_basis,
    vol_surface,
    chol_factor,
    exposure_load,
    reset_load,
    strikes,
    bucket_weight,
    bucket_start,
    generator,
    point_ids,
):
    paths = saved_paths.reshape(STEPS, NF)
    bstart = bucket_start.reshape(1, NB)
    rows = (reset_load, strikes.reshape(1, NB), bucket_weight.reshape(1, NB), bstart)

    moved = [lax.ppermute(pca_basis, ALL, basis_moves(d)) for d in range(2)]
    chunks = STEPS // CHUNK
    row_spec = pl.BlockSpec((CHUNK, NF), lambda i: (i, 0))
    square = full((NF, NF))
    vol_a = vol_surface[: STEPS // 2].astype(BF)
    vol_b = vol_surface[STEPS // 2 :].astype(BF)
    y_own = call(
        margin_kernel,
        (
            point_ids, paths, vol_surface, chol_factor, generator.reshape(1, NF), exposure_load,
            reset_load, bstart,
        ),
        [((2, STEPS), F32)],
        "margins",
        cost=(STEPS * NF * (NF + 256) * 2, 4 * MIB),
        vmem=60,
        grid=(chunks,),
        in_specs=[
            pl.BlockSpec(memory_space=pltpu.SMEM), row_spec, row_spec, square, full((1, NF)),
            full((NB, NF)), full((NB, NF)), full((1, NB)),
        ],
        out_specs=pl.BlockSpec((2, CHUNK), lambda i: (0, i)),
    )
    y0 = lax.all_gather(y_own, TM, axis=0)
    moved = lax.optimization_barrier((y0, *moved))[1:]
    pair = jnp.where(lax.axis_index("x1") == 0, jnp.stack(moved), jnp.stack(moved[::-1]))
    basis = lax.all_gather(pair, "z", axis=0, tiled=True).reshape(2, 2, 2, 2, 64, STEPS)

    s2 = [swap(vol_a, "yl"), swap(after(vol_b, y0), "yl")]
    s1 = [swap(v, "c") for v in lax.optimization_barrier((vol_a, vol_b, y0))[:2]]
    s3 = [swap(v, "c") for v in s2]

    kept, o1, o2, o3, wt, bmat = call(
        sens_kernel,
        (y0, paths, vol_surface, chol_factor, exposure_load) + rows,
        [((256, NF), F32)] + [((256, NF), BF)] * 3 + [((WROWS, STEPS), BF), ((WROWS, NF), BF)],
        "sensitivities",
        cost=(STEPS * NF * (NF + 256) * 2, 5 * MIB),
        grid=(chunks,),
    )
    g1, g2, g3 = (shift_x(o, d + 1) for d, o in enumerate((o1, o2, o3)))

    ck, cs = call(
        chol_kernel,
        (after(wt, pair), bmat, paths, vol_surface),
        [((256, NF), F32)] * 2,
        "chol_term",
        cost=(STEPS * NF * (NF + 256) * 2, 5 * MIB),
        grid=(chunks,),
        in_specs=[full((WROWS, STEPS)), full((WROWS, NF)), row_spec, row_spec],
        scratch=[pltpu.VMEM((NF, NF), F32)],
    )
    ck, cs = call(
        chol_split_kernel, (ck, swap(cs, "c")), [((128, NF), F32)] * 2, "chol_split", cost=(0, MIB)
    )
    cg = swap(cs, "yl")

    peers = [(a * 2 + b, (1 - a) * 2 + 1 - b) for a in range(2) for b in range(2)]
    y = exchange(jnp.broadcast_to(y0[None], (GROUP,) + y0.shape), PEERS)
    cols, radj = call(
        points_kernel,
        (y,) + rows,
        [((BLOCKS, STEPS, 2 * GROUP), F32), ((GROUP, NB, NF), F32)],
        "points",
        cost=(0, 6 * MIB),
    )

    kept = after(kept, y)
    parts = call(
        sum_x_kernel, (kept, g1, g2, g3, ck, cg), [((8, 48, NF), BF)], "sum_x", cost=(0, 2 * MIB)
    )
    parts = after(exchange(parts, "z"), cols)
    part = call(sum_z_kernel, (parts,), [((48, NF), F32)], "sum_z", cost=(0, MIB // 2))
    got = swap(part, "yh")
    total = call(total_kernel, (part, got), [((8, 48, NF), BF)], "totals", cost=(0, MIB // 2))
    mine = call(
        gather_z_kernel, (exchange(total, "z"),), [((384, NF), BF)], "gather_z", cost=(0, MIB)
    )
    own, o1, o2, o3 = call(
        adjoint_kernel,
        (basis, vol_surface, *s1, *s2, *s3, cols, radj, chol_factor, exposure_load, bstart),
        [((ROWS, NF), F32)] + [((ROWS, NF), BF)] * 3,
        "adjoints",
        cost=(7 * STEPS * STEPS * NF * 2, 12 * MIB),
        vmem=56,
        in_specs=[pl.BlockSpec(memory_space=pl.ANY)] * 8
        + [full(cols.shape), full(radj.shape), square, full((NB, NF)), full((1, NB))],
        scratch=[
            pltpu.VMEM((2, STEPS, GROUP * NF), BF),
            pltpu.VMEM((ROWS, GROUP * NF), F32),
            pltpu.VMEM((BLOCKS, 2, 2, 64, STEPS), BF),
            pltpu.VMEM((STEPS, NF), F32),
            pltpu.VMEM((BLOCKS - 1, STEPS, NF), BF),
            pltpu.SemaphoreType.DMA((11,)),
        ],
    )
    vol_greeks, quarter = call(
        greeks_kernel,
        [after(mine, own)] + [shift_x(mine, d) for d in range(1, 4)],
        [((STEPS, NF), F32), ((128, NF), BF)],
        "greeks",
        cost=(0, 4 * MIB),
    )
    halved = call(
        chol_half_kernel, (quarter, swap(quarter, "yl")), [((256, NF), BF)], "chol_half", cost=(0, MIB)
    )
    chol_greeks = call(
        chol_out_kernel, (halved, swap(halved, "c")), [((NF, NF), F32)], "chol_out", cost=(0, 2 * MIB)
    )

    normals = call(
        normals_kernel,
        (own, swap(o1, "x0"), swap(o2, "yh"), lax.ppermute(o3, PEERS, peers)),
        [((STEPS * 4, 128), F32)],
        "normals",
        cost=(0, 4 * MIB),
    )
    return normals.reshape(STEPS, 1, NF), vol_greeks, chol_greeks


def solution(mesh):
    split = Mesh(mesh.devices.reshape(2, 2, 2, 8, 2, 2), ALL)
    return jax.shard_map(
        body,
        mesh=split,
        in_specs=(
            P(TM, PTS, None),
            P(PTS, TM),
            P(TM, None),
            P(),
            P(),
            P(),
            P(),
            P(),
            P(),
            P(),
            P(PTS),
        ),
        out_specs=(P(TM, PTS, None), P(TM, None), P()),
        check_vma=False,
    )
```

```python
import jax
import jax.numpy as jnp
from jax import lax
from jax.experimental import pallas as pl
from jax.experimental.pallas import tpu as pltpu
from jax.sharding import Mesh, PartitionSpec as P

BF = jnp.bfloat16
F32 = jnp.float32
I32 = jnp.int32
ALL = ("yl", "c", "yh", "z2", "z1", "z0", "x1", "x0")
TM = ("yl", "c")
X = ("x1", "x0")
Z = ("z2", "z1", "z0")
PTS = ("yh",) + Z + X
PEERS = ("yh", "z0")
NB = 32
STEPS = 1024
BLOCKS = 4
CHUNK = 256
NF = 512
GROUP = 4
ROWS = STEPS // GROUP
WROWS = 5 * NB
MIB = 1024 * 1024

NN = (((1,), (0,)), ((), ()))
NT = (((1,), (1,)), ((), ()))
TN = (((0,), (0,)), ((), ()))


def dot(a, b, dims):
    return lax.dot_general(a, b, dims, preferred_element_type=F32)


def split2(x):
    hi = x.astype(BF)
    return hi, (x - hi.astype(F32)).astype(BF)


def split3(x):
    hi, mid = split2(x)
    return hi, mid, (x - hi.astype(F32) - mid.astype(F32)).astype(BF)


def column(row, shift=0):
    i = lax.broadcasted_iota(I32, (NB, NB), 0)
    j = lax.broadcasted_iota(I32, (NB, NB), 1)
    return jnp.sum(jnp.where(j == i + shift, row, 0), axis=1, keepdims=True)


def bucket_ends(bstart):
    start = column(bstart)
    last = lax.broadcasted_iota(I32, (NB, 1), 0) == NB - 1
    return start, jnp.where(last, BLOCKS * STEPS, column(bstart, 1))


def bucket_rows(bstart):
    i = lax.broadcasted_iota(I32, (NB, NB), 0)
    j = lax.broadcasted_iota(I32, (NB, NB), 1)
    nxt = jnp.sum(jnp.where(i == j + 1, column(bstart), 0), axis=0, keepdims=True)
    last = lax.broadcasted_iota(I32, (1, NB), 1) == NB - 1
    nxt = jnp.where(last, BLOCKS * STEPS, nxt)
    return jnp.concatenate([bstart] * 4, axis=1), jnp.concatenate([nxt] * 4, axis=1)


def one_hots(first_step, count, start, nxt):
    t = first_step + lax.broadcasted_iota(I32, (NB, count), 1)
    member = jnp.where((t >= start) & (t < nxt), 1.0, 0.0)
    at_start = jnp.where(t == start, 1.0, 0.0)
    return member, at_start


def own_block():
    return lax.axis_index("yl") * 2 + lax.axis_index("c")


def margin_kernel(pid, paths, vol, chol, gen, load, reset, bstart, out, vol_bf):
    i = pl.program_id(0)
    vol_bf[...] = vol[...].astype(BF)
    low = (pid[0] * (gen[...] & 1023)) & 1048575
    high = ((pid[0] * (gen[...] >> 10)) & 1023) << 10
    residue = (low + high) & 1048575
    start_state = 0.5 * 3.4641016151377544 * ((residue.astype(F32) + 0.5) / 1048576.0 - 0.5)
    state = start_state + vol[...] * dot(paths[...], chol[...], NT)
    s1, s2 = split2(state)
    l1, l2 = split2(load[...])
    r1, r2 = split2(reset[...])
    none = jnp.zeros_like(l1)
    by_bucket = dot(s1, jnp.concatenate([l1, l2, r1, r2], axis=0), NT) + dot(
        s2, jnp.concatenate([l1, none, r1, none], axis=0), NT
    )
    start, nxt = bucket_rows(bstart[...])
    t = own_block() * STEPS + i * CHUNK + lax.broadcasted_iota(I32, (CHUNK, 4 * NB), 0)
    lane = lax.broadcasted_iota(I32, (CHUNK, 4 * NB), 1)
    margin = jnp.where((lane < 2 * NB) & (t >= start) & (t < nxt), by_bucket, 0.0)
    term = jnp.where((lane >= 2 * NB) & (t == start), by_bucket, 0.0)
    margin = jnp.sum(margin, axis=1, keepdims=True)
    term = jnp.sum(term, axis=1, keepdims=True)
    both = jnp.where(lane == 0, margin, jnp.where(lane == 1, term, 0.0))
    out[...] = jnp.transpose(both)[0:2]


def group_index():
    return lax.axis_index("yh") * 2 + lax.axis_index("z0")


def bucket_values(y, hots, strikes, weight):
    term = sum(jnp.sum(hots[b][1] * y(b)[1:2], axis=1, keepdims=True) for b in range(BLOCKS))
    offset = term - strikes
    total = jnp.zeros((NB, 1), F32)
    rows = []
    for b in range(BLOCKS):
        row = step_sens(y(b), hots[b][0], offset, weight)
        total = total + jnp.sum(hots[b][0] * row, axis=1, keepdims=True)
        rows.append(row)
    return rows, total, offset


def step_sens(y, member, offset, weight):
    margin = y[0:1] + jnp.sum(member * offset, axis=0, keepdims=True)
    gain = jnp.sum(member * weight, axis=0, keepdims=True)
    return gain * jax.nn.sigmoid(margin)


def all_hots(start, nxt):
    return [one_hots(b * STEPS, STEPS, start, nxt) for b in range(BLOCKS)]


def x_index():
    return lax.axis_index("x1") * 2 + lax.axis_index("x0")


def sens_kernel(
    y, paths, vol, chol, load, reset, strikes, weight, bstart, kept, o1, o2, o3, wt, bmat
):
    i = pl.program_id(0)

    @pl.when(i == 0)
    def _():
        start, nxt = bucket_ends(bstart[...])
        w = column(weight[...])
        own = own_block()
        _, total, offset = bucket_values(
            lambda b: y[b], all_hots(start, nxt), column(strikes[...]), w
        )
        member, at_start = one_hots(own * STEPS, STEPS, start, nxt)
        m1, m2 = split2(member * step_sens(y[own], member, offset, w))
        a = at_start.astype(BF)
        wt[...] = jnp.concatenate([m1, m1, m2, a, a], axis=0)
        l1, l2 = split2(load[...])
        r1, r2 = split2(total * reset[...])
        bmat[...] = jnp.concatenate([l1, l2, l1, r1, r2], axis=0)

    at = pl.ds(pl.multiple_of(lax.rem(x_index() + i, 4) * CHUNK, CHUNK), CHUNK)
    term = dot(wt[:, at], bmat[...], TN) * dot(paths[at, :], chol[...], NT)

    @pl.when(i == 0)
    def _():
        kept[...] = term

    for k, o in enumerate((o1, o2, o3)):

        @pl.when(i == k + 1)
        def _(o=o):
            o[...] = term.astype(BF)


def chol_kernel(wt, bmat, paths, vol, kept, sent, acc):
    i = pl.program_id(0)
    at = pl.ds(pl.multiple_of(i * CHUNK, CHUNK), CHUNK)
    scaled = (vol[...] * dot(wt[:, at], bmat[...], TN)).astype(BF)
    new = dot(scaled, paths[...], TN)

    @pl.when(i == 0)
    def _():
        acc[...] = new

    @pl.when(i > 0)
    def _():
        acc[...] += new

    @pl.when(i == STEPS // CHUNK - 1)
    def _():
        c = lax.axis_index("c")
        kept[...] = acc[pl.ds(pl.multiple_of(c * 256, 256), 256), :]
        sent[...] = acc[pl.ds(pl.multiple_of((1 - c) * 256, 256), 256), :]


def chol_split_kernel(own, got, kept, sent):
    yl = lax.axis_index("yl")
    for o, at in ((kept, yl), (sent, 1 - yl)):
        rows = pl.ds(pl.multiple_of(at * 128, 128), 128)
        o[...] = own[rows, :] + got[rows, :]


def sum_x_kernel(kept, g1, g2, g3, c0, c1, out):
    for z in range(8):
        rows = slice(z * 32, z * 32 + 32)
        v = kept[rows, :] + g1[rows, :].astype(F32) + g2[rows, :].astype(F32)
        v = v + g3[rows, :].astype(F32)
        rows = slice(z * 16, z * 16 + 16)
        out[z] = jnp.concatenate([v, c0[rows, :] + c1[rows, :]], axis=0).astype(BF)


def sum_z_kernel(parts, out):
    total = parts[0].astype(F32)
    for k in range(1, parts.shape[0]):
        total = total + parts[k].astype(F32)
    out[...] = total


def total_kernel(own, got, out):
    total = (own[...] + got[...]).astype(BF)
    for z in range(8):
        out[z] = total


def gather_z_kernel(parts, out):
    for z in range(8):
        out[z * 32 : z * 32 + 32, :] = parts[z, 0:32]
        out[256 + z * 16 : 272 + z * 16, :] = parts[z, 32:48]


def greeks_kernel(own, g1, g2, g3, vol_out, chol_out):
    chol = jnp.zeros((128, NF), F32)
    for d, g in enumerate((own, g1, g2, g3)):
        at = pl.ds(pl.multiple_of(lax.rem(x_index() + 4 - d, 4) * 256, 256), 256)
        vol_out[at, :] = g[0:256, :].astype(F32)
        chol = chol + g[256:384, :].astype(F32)
    chol_out[...] = chol.astype(BF)


def chol_half_kernel(own, got, out):
    yl = lax.axis_index("yl")
    for g, at in ((own, yl), (got, 1 - yl)):
        out[pl.ds(pl.multiple_of(at * 128, 128), 128), :] = g[...]


def chol_out_kernel(own, got, out):
    c = lax.axis_index("c")
    for g, at in ((own, c), (got, 1 - c)):
        out[pl.ds(pl.multiple_of(at * 256, 256), 256), :] = g[...].astype(F32) / (BLOCKS * STEPS)


def points_kernel(y, reset, strikes, weight, bstart, cols, radj):
    start, nxt = bucket_ends(bstart[...])
    hots = all_hots(start, nxt)
    w, k = column(weight[...]), column(strikes[...])
    rows = [[] for _ in range(BLOCKS)]
    for q in range(GROUP):
        g = group_index() ^ q
        sens, total, _ = bucket_values(lambda b: y[g, b], hots, k, w)
        radj[q] = total * reset[...]
        for b in range(BLOCKS):
            rows[b].append(sens[b])
    for b in range(BLOCKS):
        cols[b] = jnp.transpose(jnp.concatenate(rows[b] + rows[b], axis=0))


def adjoint_kernel(
    b0, b1, b2, b3, vol_hbm, s1, s2a, s2b, s3a, s3b, cols, radj, chol, load, bstart,
    own, o1, o2, o3, scaled, acc, basis, vol, vols, vol_load, sems,
):
    half = STEPS // 2
    copies = [[pltpu.make_async_copy(vol_hbm, vol, sems.at[0])]]
    copies.append([pltpu.make_async_copy(s1, vols.at[0], sems.at[1])])
    for r, pair in enumerate(((s2a, s2b), (s3a, s3b))):
        copies.append(
            [
                pltpu.make_async_copy(p, vols.at[r + 1, pl.ds(h * half, half)], sems.at[2 + 2 * r + h])
                for h, p in enumerate(pair)
            ]
        )
    z2, z1, x = lax.axis_index("z2"), lax.axis_index("z1"), x_index()
    for r in range(BLOCKS):
        piece = ((r & 1) ^ z1) * 2 + ((r >> 1) ^ z2)
        for d, b in enumerate((b0, b1, b2, b3)):
            place = basis.at[r, lax.rem(x + 4 - d, 4)]
            copies[r].append(pltpu.make_async_copy(b.at[piece], place, sems.at[6 + 4 * r + d]))
        for copy in copies[r]:
            copy.start()
    start, nxt = bucket_ends(bstart[...])
    load_parts = jnp.concatenate(split3(load[...]), axis=0)
    at_resets = jnp.zeros((ROWS, NB), F32)
    vol_resets = jnp.zeros((NB, NF), F32)
    for r in range(BLOCKS + 1):
        if r < BLOCKS:
            for copy in copies[r]:
                copy.wait()
            b = own_block() ^ r
            member, at_start = one_hots(b * STEPS, STEPS, start, nxt)
            member, at_start = member.astype(BF), at_start.astype(BF)
            hots = jnp.concatenate([member] * 3, axis=0)
            at_resets = at_resets + dot(basis[r].reshape(ROWS, STEPS), at_start, NT)
        for q in range(GROUP):
            cut = slice(q * NF, (q + 1) * NF)
            for j in range(STEPS // CHUNK if r < BLOCKS else 0):
                rows = slice(j * CHUNK, (j + 1) * CHUNK)
                if q == 0:
                    v = vols[r - 1, rows, :] if r else vol[rows, :]
                    for h in (v,) if r else split2(v):
                        vol_resets = vol_resets + dot(at_start[:, rows], h, NN)
                    vol_load[rows, :] = v.astype(F32) * dot(hots[:, rows], load_parts, TN)
                part = vol_load[rows, :] * cols[b, rows, q : q + 1]
                scaled[r % 2, rows, cut] = part.astype(BF)
            if r:
                new = dot(basis[r - 1].reshape(ROWS, STEPS), scaled[1 - r % 2, :, cut], NN)
                acc[:, cut] = new if r == 1 else acc[:, cut] + new
    at_resets = at_resets.astype(BF)
    for q, o in enumerate((own, o1, o2, o3)):
        more = dot(at_resets, (vol_resets * radj[q]).astype(BF), NN)
        h1, h2 = split2(acc[:, q * NF : (q + 1) * NF] + more)
        o[...] = (dot(h1, chol[...], NN) + dot(h2, chol[...], NN)).astype(o.dtype)


def normals_kernel(own, g1, g2, g3, out):
    for q, g in enumerate((own, g1, g2, g3)):
        first = pl.multiple_of((group_index() ^ q) * (ROWS * 4), ROWS * 4)
        for j in range(4):
            at = pl.ds(first + j, ROWS, stride=4)
            out[at, :] = g[:, j * 128 : (j + 1) * 128].astype(F32)


def full(shape):
    return pl.BlockSpec(shape, lambda *_: (0,) * len(shape))


def call(kernel, args, outs, name, cost, vmem=40, scratch=(), **kw):
    single = len(outs) == 1
    shapes = [jax.ShapeDtypeStruct(s, d) for s, d in outs]
    spec = dict(
        in_specs=[full(a.shape) for a in args], out_specs=[full(s.shape) for s in shapes], grid=(1,)
    )
    spec.update(kw)
    if single and isinstance(spec["out_specs"], list):
        spec["out_specs"] = spec["out_specs"][0]
    return pl.pallas_call(
        kernel,
        out_shape=shapes[0] if single else shapes,
        scratch_shapes=list(scratch),
        cost_estimate=pl.CostEstimate(flops=cost[0], bytes_accessed=cost[1], transcendentals=0),
        compiler_params=pltpu.CompilerParams(vmem_limit_bytes=vmem * MIB),
        name=name,
        **spec,
    )(*args)


def basis_moves(d):
    moves = []
    for yl in range(2):
        for c in range(2):
            for yh in range(2):
                for z in range(8):
                    for x in range(4):
                        src = (((yl * 2 + c) * 2 + yh) * 8 + z) * 4 + x
                        z2, z1, z0 = z >> 2, (z >> 1) & 1, z & 1
                        to_z = (yl ^ yh ^ d) * 4 + (c ^ z2) * 2 + z0
                        moves.append((src, (((yh * 2 + z2) * 2 + z1) * 8 + to_z) * 4 + x))
    return moves


def swap(x, axis):
    return lax.ppermute(x, axis, [(0, 1), (1, 0)])


def shift_x(x, d):
    return lax.ppermute(x, X, [(i, (i + d) % 4) for i in range(4)])


def exchange(x, axes):
    return lax.all_to_all(x, axes, split_axis=0, concat_axis=0, tiled=True)


def after(x, *first):
    return lax.optimization_barrier((x,) + first)[0]


def body(
    saved_paths,
    pca_basis,
    vol_surface,
    chol_factor,
    exposure_load,
    reset_load,
    strikes,
    bucket_weight,
    bucket_start,
    generator,
    point_ids,
):
    paths = saved_paths.reshape(STEPS, NF)
    bstart = bucket_start.reshape(1, NB)
    rows = (reset_load, strikes.reshape(1, NB), bucket_weight.reshape(1, NB), bstart)

    moved = [lax.ppermute(pca_basis, ALL, basis_moves(d)) for d in range(2)]
    chunks = STEPS // CHUNK
    row_spec = pl.BlockSpec((CHUNK, NF), lambda i: (i, 0))
    square = full((NF, NF))
    y_own, vol_bf = call(
        margin_kernel,
        (
            point_ids, paths, vol_surface, chol_factor, generator.reshape(1, NF), exposure_load,
            reset_load, bstart,
        ),
        [((2, STEPS), F32), ((STEPS, NF), BF)],
        "margins",
        cost=(STEPS * NF * (NF + 256) * 2, 4 * MIB),
        vmem=60,
        grid=(chunks,),
        in_specs=[
            pl.BlockSpec(memory_space=pltpu.SMEM), row_spec, row_spec, square, full((1, NF)),
            full((NB, NF)), full((NB, NF)), full((1, NB)),
        ],
        out_specs=[pl.BlockSpec((2, CHUNK), lambda i: (0, i)), row_spec],
    )
    y0 = lax.all_gather(y_own, TM, axis=0)
    y0, *moved = lax.optimization_barrier((y0, *moved))
    moved = jnp.stack(moved)

    kept, o1, o2, o3, wt, bmat = call(
        sens_kernel,
        (y0, paths, vol_surface, chol_factor, exposure_load) + rows,
        [((256, NF), F32)] + [((256, NF), BF)] * 3 + [((WROWS, STEPS), BF), ((WROWS, NF), BF)],
        "sensitivities",
        cost=(STEPS * NF * (NF + 256) * 2, 5 * MIB),
        grid=(chunks,),
    )
    g1, g2, g3 = (shift_x(o, d + 1) for d, o in enumerate((o1, o2, o3)))

    ck, cs = call(
        chol_kernel,
        (wt, bmat, paths, vol_surface),
        [((256, NF), F32)] * 2,
        "chol_term",
        cost=(STEPS * NF * (NF + 256) * 2, 5 * MIB),
        grid=(chunks,),
        in_specs=[full((WROWS, STEPS)), full((WROWS, NF)), row_spec, row_spec],
        scratch=[pltpu.VMEM((NF, NF), F32)],
    )
    ck, cs = call(
        chol_split_kernel, (ck, swap(cs, "c")), [((128, NF), F32)] * 2, "chol_split", cost=(0, MIB)
    )
    cg = swap(cs, "yl")

    vol_a, vol_b = vol_bf[: STEPS // 2], vol_bf[STEPS // 2 :]
    s2 = [swap(after(vol_a, y0), "yl"), swap(after(vol_b, cg), "yl")]
    s1 = swap(after(vol_bf, cg), "c")
    s3 = [swap(v, "c") for v in s2]
    peers = [(a * 2 + b, (1 - a) * 2 + 1 - b) for a in range(2) for b in range(2)]
    y = exchange(jnp.broadcast_to(y0[None], (GROUP,) + y0.shape), PEERS)
    cols, radj = call(
        points_kernel,
        (y,) + rows,
        [((BLOCKS, STEPS, 2 * GROUP), F32), ((GROUP, NB, NF), F32)],
        "points",
        cost=(0, 6 * MIB),
    )

    quad = jnp.concatenate([moved, swap(moved, "z1")])

    kept = after(kept, s2[0], y)
    parts = call(
        sum_x_kernel, (kept, g1, g2, g3, ck, cg), [((8, 48, NF), BF)], "sum_x", cost=(0, 2 * MIB)
    )
    basis = [quad] + [shift_x(after(quad, parts), d) for d in range(1, 4)]
    parts = after(exchange(parts, Z), cols, s2[1])
    part = call(sum_z_kernel, (parts,), [((48, NF), F32)], "sum_z", cost=(0, MIB // 2))
    got = after(swap(part, "yh"), basis[1], basis[3])
    total = call(total_kernel, (part, got), [((8, 48, NF), BF)], "totals", cost=(0, MIB // 2))
    own, o1, o2, o3 = call(
        adjoint_kernel,
        (*basis, vol_surface, s1, *s2, *s3, cols, radj, chol_factor, exposure_load, bstart),
        [((ROWS, NF), F32)] + [((ROWS, NF), BF)] * 3,
        "adjoints",
        cost=(7 * STEPS * STEPS * NF * 2, 12 * MIB),
        vmem=56,
        in_specs=[pl.BlockSpec(memory_space=pl.ANY)] * 10
        + [full(cols.shape), full(radj.shape), square, full((NB, NF)), full((1, NB))],
        scratch=[
            pltpu.VMEM((2, STEPS, GROUP * NF), BF),
            pltpu.VMEM((ROWS, GROUP * NF), F32),
            pltpu.VMEM((BLOCKS, 4, 64, STEPS), BF),
            pltpu.VMEM((STEPS, NF), F32),
            pltpu.VMEM((BLOCKS - 1, STEPS, NF), BF),
            pltpu.VMEM((STEPS, NF), F32),
            pltpu.SemaphoreType.DMA((22,)),
        ],
    )
    mine = call(
        gather_z_kernel, (after(exchange(total, Z), basis[2]),), [((384, NF), BF)], "gather_z", cost=(0, MIB)
    )
    spread = [mine] + [shift_x(mine, d) for d in range(1, 4)]
    others = swap(o1, "z0"), swap(o2, "yh"), lax.ppermute(o3, PEERS, peers)
    spread[0] = after(mine, own)
    vol_greeks, quarter = call(
        greeks_kernel,
        spread,
        [((STEPS, NF), F32), ((128, NF), BF)],
        "greeks",
        cost=(0, 4 * MIB),
    )
    halved = call(
        chol_half_kernel, (quarter, swap(quarter, "yl")), [((256, NF), BF)], "chol_half", cost=(0, MIB)
    )
    chol_greeks = call(
        chol_out_kernel, (halved, swap(halved, "c")), [((NF, NF), F32)], "chol_out", cost=(0, 2 * MIB)
    )

    normals = call(
        normals_kernel,
        (own, *others),
        [((STEPS * 4, 128), F32)],
        "normals",
        cost=(0, 4 * MIB),
    )
    return normals.reshape(STEPS, 1, NF), vol_greeks, chol_greeks


def solution(mesh):
    split = Mesh(mesh.devices.reshape((2,) * 8), ALL)
    return jax.shard_map(
        body,
        mesh=split,
        in_specs=(
            P(TM, PTS, None),
            P(PTS, TM),
            P(TM, None),
            P(),
            P(),
            P(),
            P(),
            P(),
            P(),
            P(),
            P(PTS),
        ),
        out_specs=(P(TM, PTS, None), P(TM, None), P()),
        check_vma=False,
    )
```
